32 devices in a mesh: members: 2 (over x), tiles: 16 (over z, y, core).
Axes of the slice: x: 2, y: 2, z: 4, core: 2. Of those that a mesh axis runs over, the one named last changes fastest.
Arguments:
- atmos: float32 [60, 384, 1152], P('members', 'tiles'), parts along dimension 0, may hold values from -6 to 6
- water_anomaly: float32 [100, 128, 1440], P('members', 'tiles'), parts along dimension 0, may hold values from -6 to 6
- atm_flux: float32 [384, 2304], P('tiles', 'members'), parts along dimension 1, may hold values from -6 to 6
- ocean_mask: int32 [128, 1440], P('tiles'), may hold values from 0 to 1, as said below
- air_mixing_numbers: float32 [384, 1152], P('tiles'), may hold values from 0.02 to 0.24
- ocean_kappa: float32 [128, 1440], P('tiles'), may hold values from 0.02 to 0.24
- air_vertical_operator: float32 [30, 30], replicated, may hold values from -1.5 to 1.5
- ocean_column: float32 [50, 50], replicated, may hold values from -1.5 to 1.5
- a2o_source: int32 [16, 16, 48], P('tiles'), may hold values from 0 to 215
- a2o_target: int32 [16, 16, 48], P('tiles'), may hold values from 0 to 89, as said below
- a2o_count: int32 [16, 16], P('tiles'), may hold values from 0 to 48, as said below
- a2o_weight: float32 [16, 16, 48, 128], P('tiles'), may hold values from 0.2 to 0.8
- water_air_provider: int32 [16, 16, 48], P('tiles'), may hold values from 0 to 89
- water_air_receiver: int32 [16, 16, 48], P('tiles'), may hold values from 0 to 215, as said below
- water_air_live_tally: int32 [16, 16], P('tiles'), may hold values from 0 to 48, as said below
- water_air_overlay_share: float32 [16, 16, 48, 128], P('tiles'), may hold values from 0.2 to 0.8
Outputs:
- atmos_next: float32 [60, 384, 1152], P('members', 'tiles'), parts along dimension 0
- ocean_next: float32 [100, 128, 1440], P('members', 'tiles'), parts along dimension 0
- future_energy_exchange: float32 [384, 2304], P('tiles', 'members'), parts along dimension 1
The draws below stay inside these ranges and needn't reach their ends.
There are 2 independent parts, one for each index of `members`. The reference program is written for one: setup_inputs(seed, part) draws one part's arguments, and reference() takes and returns one part's arrays. A program takes and returns all parts, laid end to end along the dimension named above; an argument that names none is the same for every part. Nothing has to cross between parts.
Inputs may be any that keep to these rules, and one draw needn't show every extreme that they name: `ocean_mask`: 1 marks sea; in each tile every block from some block number on is all land. `a2o_count`: with N the number of tiles, list the tile offsets 0, N - 1, N // 2 and then 1, 2, 3 and so on without repeats; tile d has live slots only from tiles d plus the first 5 of these offsets, modulo N. `a2o_target`: each destination block gets 2 live slots or none; blocks holding sea get 2. `water_air_live_tally`: with N the number of tiles, list the tile offsets 0, N - 1, N // 2 and then 1, 2, 3 and so on without repeats; tile d has live slots only from tiles d plus the first 10 of these offsets, modulo N. `water_air_receiver`: each destination block gets exactly 2 live slots.
All inputs are finite; a program needn't handle non-finite values.
Results may differ from the reference program's by a relative error of at most 0.0003.
Values sent between devices are 32-bit elements; how exact they have to be, the bound alone decides.
A program may use at most 128 MiB of HBM per device.

```python
import math
import jax
import jax.numpy as jnp
from jax import lax

NLON_A = 1152
NLON_O = 1440
ROWS_O = 8
LEV_A = 30
LEV_O = 50
PATCH_SIZE = 128
K = 2
CAP = 48
NLAT_A = 384
NLAT_O = 128
AB = 216
OB = 90
N_TILES = 16


def offset_inverse():
    leading = [0, N_TILES - 1, N_TILES // 2]
    ordered = leading + [value for value in range(N_TILES) if value not in leading]
    return jnp.array([ordered.index(value) for value in range(N_TILES)], dtype=jnp.int32)


def ocean_live(key):
    key = jax.random.fold_in(key, 501)
    first, second = jax.random.split(key)
    counts = jax.random.randint(first, (N_TILES,), OB // 4, OB + 1)
    chosen = jax.random.randint(second, (), 0, N_TILES)
    return jnp.where(jnp.arange(N_TILES) == chosen, OB, counts).astype(jnp.int32)


def slot_lists(key, salt, live_dest, dest_blocks):
    key = jax.random.fold_in(key, salt)
    first, second, third = jax.random.split(key, 3)
    entries = live_dest * K
    offsets = jnp.arange(N_TILES, dtype=jnp.int32)
    slots = jnp.arange(CAP, dtype=jnp.int32)
    skip = jax.random.randint(third, (N_TILES,), 0, CAP + 1).astype(jnp.int32)
    upper = jnp.clip(skip[:, None] + entries[:, None] - offsets[None, :] * CAP, 0, CAP)
    lower = jnp.clip(skip[:, None] - offsets[None, :] * CAP, 0, CAP)
    count_by_q = (upper - lower).astype(jnp.int32)
    prefix = jnp.cumsum(count_by_q, axis=1) - count_by_q
    live = slots[None, None, :] < count_by_q[:, :, None]
    index = prefix[:, :, None] + slots[None, None, :]
    rotate = jax.random.randint(first, (N_TILES, 1, 1), 0, dest_blocks)
    wanted = (index + rotate) % live_dest[:, None, None]
    filler = jax.random.randint(second, (N_TILES, N_TILES, CAP), 0, dest_blocks)
    by_q = jnp.where(live, wanted, filler).astype(jnp.int32)
    inverse = offset_inverse()
    q_index = inverse[(offsets[None, :] - offsets[:, None]) % N_TILES]
    rows = offsets[:, None]
    return (by_q[rows, q_index], count_by_q[rows, q_index])


def draw_ocean_mask(key, part):
    live = ocean_live(key)
    key = jax.random.fold_in(key, 1001)
    cells = ROWS_O * NLON_O
    water_entries = jax.random.randint(key, (N_TILES, cells), 0, 5) != 0
    block = jnp.arange(cells, dtype=jnp.int32) // PATCH_SIZE
    mask = jnp.logical_and(water_entries, block[None, :] < live[:, None])
    return mask.astype(jnp.int32).reshape(NLAT_O, NLON_O)


def draw_a2o_source(key, part):
    key = jax.random.fold_in(key, 801)
    return jax.random.randint(key, (N_TILES, N_TILES, CAP), 0, AB).astype(jnp.int32)


def draw_a2o_target(key, part):
    live = ocean_live(key)
    target, count = slot_lists(key, 601, live, OB)
    return target


def draw_a2o_count(key, part):
    live = ocean_live(key)
    target, count = slot_lists(key, 601, live, OB)
    return count


def draw_water_air_provider(key, part):
    live = ocean_live(key)
    key = jax.random.fold_in(key, 901)
    return jax.random.randint(key, (N_TILES, N_TILES, CAP), 0, live[:, None, None]).astype(jnp.int32)


def draw_water_air_receiver(key, part):
    live = jnp.full((N_TILES,), AB, jnp.int32)
    target, count = slot_lists(key, 701, live, AB)
    return target


def draw_water_air_live_tally(key, part):
    live = jnp.full((N_TILES,), AB, jnp.int32)
    target, count = slot_lists(key, 701, live, AB)
    return count


def steps_of(rng, shape, pieces, smallest, top_value):
    def one(position, parts):
        draws = jax.random.uniform(jax.random.fold_in(jax.random.fold_in(rng, 6), position), (parts,), jnp.float32, smallest / len(pieces), top_value / len(pieces))
        return jnp.repeat(jnp.exp(draws), shape[position] // parts).reshape((-1,) + (1,) * (len(shape) - position - 1))

    level = one(*pieces[0])
    for cut in pieces[1:]:
        level = level * one(*cut)
    return level


def centred(stream_key, shape, spread, reach, cuts=(), kind=jnp.bfloat16):
    values = jax.random.normal(stream_key, shape, jnp.float32) * spread
    if len(cuts) > 0:
        values = steps_of(stream_key, shape, cuts, -0.22, 0.18) * values
    return jnp.clip(values, min=-reach, max=reach).astype(kind)


def setup_inputs(seed: int = 0, part: int = 0) -> dict:
    splits = jax.random.split(jax.random.key(seed), 17)
    own_keys = jax.random.split(jax.random.fold_in(splits[16], part), 17)
    atmos = centred(own_keys[0], (LEV_A, NLAT_A, NLON_A), 1.0, 6.0, ((1, 16),), jnp.float32)
    water_anomaly = centred(own_keys[1], (LEV_O, NLAT_O, NLON_O), 1.0, 6.0, ((1, 16),), jnp.float32)
    atm_flux = centred(own_keys[2], (NLAT_A, NLON_A), 1.0, 6.0, ((0, 16),), jnp.float32)
    ocean_mask = draw_ocean_mask(jax.random.fold_in(splits[16], 71), part)
    air_mixing_numbers = jnp.clip(jnp.exp(math.log(0.24) - 2.4849066 * jax.random.uniform(splits[4], (NLAT_A, NLON_A), jnp.float32) ** steps_of(splits[4], (NLAT_A, NLON_A), ((0, 16),), -0.2, 0.2)), 0.02, 0.24)
    ocean_kappa = jnp.clip(jnp.exp(math.log(0.24) - 2.4849066 * jax.random.uniform(splits[5], (NLAT_O, NLON_O), jnp.float32) ** steps_of(splits[5], (NLAT_O, NLON_O), ((0, 16),), -0.2, 0.2)), 0.02, 0.24)
    air_vertical_operator = centred(splits[6], (LEV_A, LEV_A), 0.1, 1.5, (), jnp.float32)
    ocean_column = centred(splits[7], (LEV_O, LEV_O), 0.1, 1.5, (), jnp.float32)
    a2o_source = draw_a2o_source(jax.random.fold_in(splits[16], 71), part)
    a2o_target = draw_a2o_target(jax.random.fold_in(splits[16], 71), part)
    a2o_count = draw_a2o_count(jax.random.fold_in(splits[16], 71), part)
    a2o_weight = jnp.clip(0.2 + 0.6 * jax.random.uniform(splits[11], (N_TILES, N_TILES, CAP, PATCH_SIZE), jnp.float32) ** steps_of(splits[11], (N_TILES, N_TILES, CAP, PATCH_SIZE), ((0, 16),), -0.2, 0.2), 0.2, 0.8)
    water_air_provider = draw_water_air_provider(jax.random.fold_in(splits[16], 71), part)
    water_air_receiver = draw_water_air_receiver(jax.random.fold_in(splits[16], 71), part)
    water_air_live_tally = draw_water_air_live_tally(jax.random.fold_in(splits[16], 71), part)
    water_air_overlay_share = jnp.clip(0.2 + 0.6 * jax.random.uniform(splits[15], (N_TILES, N_TILES, CAP, PATCH_SIZE), jnp.float32) ** steps_of(splits[15], (N_TILES, N_TILES, CAP, PATCH_SIZE), ((0, 16),), -0.2, 0.2), 0.2, 0.8)
    return dict(atmos=atmos, water_anomaly=water_anomaly, atm_flux=atm_flux, ocean_mask=ocean_mask, air_mixing_numbers=air_mixing_numbers, ocean_kappa=ocean_kappa, air_vertical_operator=air_vertical_operator, ocean_column=ocean_column, a2o_source=a2o_source, a2o_target=a2o_target, a2o_count=a2o_count, a2o_weight=a2o_weight, water_air_provider=water_air_provider, water_air_receiver=water_air_receiver, water_air_live_tally=water_air_live_tally, water_air_overlay_share=water_air_overlay_share)


AIR_EXCHANGER = 0.3
COUPLE_OCEAN = 0.5


def remap_between_grids(blocks, source, target, count, weight, dest_count):
    tile_ids = jnp.arange(N_TILES, dtype=jnp.int32)
    slot_ids = jnp.arange(CAP, dtype=jnp.int32)
    block_ids = jnp.arange(dest_count, dtype=jnp.int32)

    def one_tile(dest):
        picks = source[:, dest, :]
        values = blocks[tile_ids[:, None], picks]
        live = (slot_ids[None, :] < count[dest][:, None]).astype(jnp.float32)
        terms = weight[dest] * values * live[:, :, None]
        onehot = (target[dest][:, :, None] == block_ids).astype(jnp.float32)
        return jnp.einsum("scj,scb->jb", onehot, terms, precision=lax.Precision.HIGHEST)

    return lax.map(one_tile, tile_ids)


def air_advance_interval(widened_array, mixing_coefficient, vertical_linear_system, skin_water_warmth):
    interior_points = widened_array[:, 1:-1]
    beside = widened_array[:, 2:] + widened_array[:, :-2] + jnp.roll(interior_points, 1, 2) + jnp.roll(interior_points, -1, 2)
    mixed = jnp.einsum("kl,lyx->kyx", vertical_linear_system, interior_points, precision=lax.Precision.HIGHEST)
    advanced_condition = interior_points + mixing_coefficient * (beside - 4.0 * interior_points) + mixed
    bottom_layer = advanced_condition[-1] + AIR_EXCHANGER * (skin_water_warmth - interior_points[-1])
    return jnp.concatenate([advanced_condition[:-1], bottom_layer[None]], 0)


def ocean_advance(widened_array, mixing_coefficient, vertical_linear_system, water_entries, flux):
    interior_points = widened_array[:, 1:-1]
    beside = widened_array[:, 2:] + widened_array[:, :-2] + jnp.roll(interior_points, 1, 2) + jnp.roll(interior_points, -1, 2)
    mixed = jnp.einsum("kl,lyx->kyx", vertical_linear_system, interior_points, precision=lax.Precision.HIGHEST)
    advanced_condition = interior_points + water_entries * (mixing_coefficient * (beside - 4.0 * interior_points) + mixed)
    surface = advanced_condition[0] + water_entries * COUPLE_OCEAN * flux
    return jnp.concatenate([surface[None], advanced_condition[1:]], 0)


def filler_lines(current_condition):
    return jnp.pad(current_condition, ((0, 0), (1, 1), (0, 0)))


def reference(atmos, water_anomaly, atm_flux, ocean_mask, air_mixing_numbers, ocean_kappa, air_vertical_operator, ocean_column,
              a2o_source, a2o_target, a2o_count, a2o_weight, water_air_provider, water_air_receiver, water_air_live_tally, water_air_overlay_share):
    water_entries = ocean_mask.astype(jnp.float32)
    skin_water_warmth = water_anomaly[0] * water_entries
    water_warmth_on_air = remap_between_grids(skin_water_warmth.reshape(N_TILES, -1, PATCH_SIZE), water_air_provider, water_air_receiver, water_air_live_tally,
                         water_air_overlay_share, AB).reshape(NLAT_A, NLON_A)
    flux_on_ocean = remap_between_grids(atm_flux.reshape(N_TILES, -1, PATCH_SIZE), a2o_source, a2o_target, a2o_count,
                          a2o_weight, OB).reshape(NLAT_O, NLON_O)
    current_condition = atmos
    for step in range(2):
        current_condition = air_advance_interval(filler_lines(current_condition), air_mixing_numbers, air_vertical_operator, water_warmth_on_air)
    future_energy_exchange = AIR_EXCHANGER * (water_warmth_on_air - current_condition[-1])
    ocean_next = ocean_advance(filler_lines(water_anomaly), ocean_kappa, ocean_column, water_entries, flux_on_ocean)
    return (current_condition, ocean_next, future_energy_exchange)
```

```python
import functools

import jax
import jax.numpy as jnp
from jax import lax
from jax.experimental import pallas as pl
from jax.experimental.pallas import tpu as pltpu
from jax.sharding import PartitionSpec as P

LANES = 128
ENTRIES = 2
AIR_EXCHANGER = 0.3
COUPLE_OCEAN = 0.5
VMEM_BYTES = 52 * 1024 * 1024


def round_up(value, unit):
    return -(-value // unit) * unit


def offsets_of(tiles, count):
    leading = [0, tiles - 1, tiles // 2]
    return (leading + [v for v in range(tiles) if v not in leading])[:count]


def split_product(matrix, cells):
    high = cells.astype(jnp.bfloat16).astype(jnp.float32)
    low = cells - high
    stacked = jnp.concatenate([high, low, high], axis=0).astype(jnp.bfloat16)
    return jnp.dot(matrix, stacked, preferred_element_type=jnp.float32)


def lane_iota(shape):
    return lax.broadcasted_iota(jnp.int32, shape, len(shape) - 1)


def exchange_kernel(
    dims,
    atmos, water, flux, mask, kap_a, kap_o, mat_a, mat_o,
    f_src, f_tgt, f_cnt, f_wgt, w_src, w_tgt, w_cnt, w_wgt,
    u2_out, o2_out, g_out, d_out, fl_out,
    in_a, u, u1, u2, in_o, o, o2, surf,
    f_blocks, w_blocks, f_send, w_send, f_recv, w_recv, f_wbuf, w_wbuf,
    eff, f_terms, w_terms, r_a, r_o, t_o, r_halo, g_rows, lanes_o, kap_rows,
    dma, f_ss, f_rs, w_ss, w_rs, h_ss, h_rs,
):
    n, la, ya, xa, lo, yo, xo, cap, nf, nw = dims
    lap, lop = round_up(la + 1, 8), round_up(lo, 8)
    xop = round_up(xo, LANES)
    tail = xo % LANES
    ja, jo = xa // LANES, xop // LANES
    me = lax.axis_index("tiles")
    offs = offsets_of(n, nw)

    def source_of(q):
        return lax.rem(me + offs[q], n)

    def dest_of(q):
        return lax.rem(me + (n - offs[q]), n)

    barrier = pltpu.get_barrier_semaphore()
    for q in range(1, nw):
        pl.semaphore_signal(barrier, inc=1, device_id={"tiles": source_of(q)})

    surf_copy = pltpu.make_async_copy(water.at[0], surf, dma.at[0])
    surf_copy.start()
    groups = ya // 8
    air_copies = [
        pltpu.make_async_copy(atmos.at[:, pl.ds(8 * i, 8), :], in_a.at[i], dma.at[1 + i])
        for i in range(groups)
    ]
    order = [0, groups - 1] + list(range(1, groups - 1))
    for i in order:
        air_copies[i].start()
    at = 1 + groups
    water_copy = pltpu.make_async_copy(water, in_o, dma.at[at])
    water_copy.start()
    at += 1
    wgt_copies = []
    for q in range(nw):
        wgt_copies.append(pltpu.make_async_copy(w_wgt.at[0, source_of(q)], w_wbuf.at[q], dma.at[at]))
        at += 1
    for q in range(nf):
        wgt_copies.append(pltpu.make_async_copy(f_wgt.at[0, source_of(q)], f_wbuf.at[q], dma.at[at]))
        at += 1
    for c in wgt_copies:
        c.start()

    for j in range(ja):
        f_blocks[pl.ds(j, ya, stride=ja), :] = flux[:, j * LANES : (j + 1) * LANES]
    surf_copy.wait()
    sea2 = mask[...].astype(jnp.float32)
    lanes_o[...] = jnp.zeros_like(lanes_o)
    lanes_o[:, 0:xo] = surf[...] * sea2
    w_blocks[...] = jnp.zeros_like(w_blocks)
    for j in range(jo):
        t_o[pl.ds(j, yo, stride=jo), :] = lanes_o[:, j * LANES : (j + 1) * LANES]
    for y in range(yo):
        first, shift = (y * xo) // LANES, (y * xo) % LANES
        tiles = t_o[y * jo : (y + 1) * jo, :]
        if shift == 0:
            w_blocks[first : first + jo, :] = tiles
        else:
            rolled = pltpu.roll(tiles, shift, 1)
            before = jnp.concatenate([w_blocks[first : first + 1, :], rolled[: jo - 1]], axis=0)
            w_blocks[first : first + jo, :] = jnp.where(
                lane_iota((jo, LANES)) < shift, before, rolled
            )

    def gather(dst, blocks, source, d):
        def body(i, carry):
            for k in range(8):
                c = i * 8 + k
                dst[pl.ds(c, 1), :] = blocks[pl.ds(source[0, d, c], 1), :]
            return carry

        lax.fori_loop(0, cap // 8, body, 0)

    for q in range(nw):
        gather(w_recv.at[0] if q == 0 else w_send.at[q - 1], w_blocks, w_src, dest_of(q))
    for q in range(nf):
        gather(f_recv.at[0] if q == 0 else f_send.at[q - 1], f_blocks, f_src, dest_of(q))

    pl.semaphore_wait(barrier, nw - 1)
    w_copies, f_copies = {}, {}
    for q in range(1, nw):
        w_copies[q] = pltpu.make_async_remote_copy(
            src_ref=w_send.at[q - 1], dst_ref=w_recv.at[q],
            send_sem=w_ss.at[q - 1], recv_sem=w_rs.at[q - 1], device_id={"tiles": dest_of(q)},
        )
    for q in range(1, nf):
        f_copies[q] = pltpu.make_async_remote_copy(
            src_ref=f_send.at[q - 1], dst_ref=f_recv.at[q],
            send_sem=f_ss.at[q - 1], recv_sem=f_rs.at[q - 1], device_id={"tiles": dest_of(q)},
        )
    for q in [2] + list(range(nw - 1, 2, -1)) + [1]:
        w_copies[q].start()
        if q in f_copies:
            f_copies[q].start()

    kap_rows[...] = jnp.zeros_like(kap_rows)

    def turn_air(i):
        air_copies[i].wait()
        for j in range(ja):
            cut = pl.ds(j * LANES, LANES)
            u[pl.ds(2 + 8 * i, 8), 0:la, cut] = jnp.swapaxes(in_a[i, :, :, cut], 0, 1)
        for r in range(8):
            u[2 + 8 * i + r, la : la + 1, :] = kap_a[8 * i + r : 8 * i + r + 1, :]
            if lap > la + 1:
                u[2 + 8 * i + r, la + 1 : lap, :] = jnp.zeros((lap - la - 1, xa), jnp.float32)

    up, down = lax.rem(me + 1, n), lax.rem(me + n - 1, n)

    def to_next(k, src, dst):
        return pltpu.make_async_remote_copy(
            src_ref=src, dst_ref=dst, send_sem=h_ss.at[k], recv_sem=h_rs.at[k],
            device_id={"tiles": up},
        )

    def to_prev(k, src, dst):
        return pltpu.make_async_remote_copy(
            src_ref=src, dst_ref=dst, send_sem=h_ss.at[k], recv_sem=h_rs.at[k],
            device_id={"tiles": down},
        )

    has_next, has_prev = me < n - 1, me > 0
    air_up = to_next(0, u.at[pl.ds(ya, 2)], u.at[pl.ds(0, 2)])
    air_down = to_prev(1, u.at[pl.ds(2, 2)], u.at[pl.ds(ya + 2, 2)])
    sea_up = to_next(2, o.at[yo], o.at[0])
    sea_down = to_prev(3, o.at[1], o.at[yo + 1])
    blk_up = to_next(4, r_a.at[pl.ds(ya * ja - 16, 16)], r_halo.at[0])
    blk_down = to_prev(5, r_a.at[pl.ds(0, 16)], r_halo.at[1])

    turn_air(0)

    @pl.when(has_prev)
    def _():
        air_down.start()

    turn_air(groups - 1)

    @pl.when(has_next)
    def _():
        air_up.start()

    water_copy.wait()
    for j in range(jo):
        width = min(LANES, xo - j * LANES)
        cut = pl.ds(j * LANES, width)
        o[pl.ds(1, yo), 0:lo, cut] = jnp.swapaxes(in_o[:, :, cut], 0, 1)
    for y in range(yo):
        o[1 + y, lo:lop, :] = jnp.zeros((lop - lo, xop), jnp.float32)
        head = o[1 + y, :, 0:LANES]
        last = o[1 + y, :, xop - LANES : xop]
        lane = lane_iota((lop, LANES))
        wrapped = jnp.where(
            lane == tail,
            pltpu.roll(head, tail, 1),
            jnp.where(lane == LANES - 1, pltpu.roll(last, LANES - tail, 1), 0.0),
        )
        o[1 + y, :, xop - LANES : xop] = jnp.where(lane < tail, last, wrapped)

    @pl.when(has_prev)
    def _():
        sea_down.start()

    @pl.when(has_next)
    def _():
        sea_up.start()

    for i in range(1, groups - 1):
        turn_air(i)

    def air_step(dst, dst_row, src, row):
        c = src[row]
        kap = u[dst_row[1], la : la + 1, :]
        beside = src[row - 1] + src[row + 1] + pltpu.roll(c, 1, 1) + pltpu.roll(c, xa - 1, 1)
        dst[dst_row[0]] = split_product(mat_a[...], c) + kap * (beside - 4.0 * c)

    def first_step(y):
        air_step(u1, (y + 1, y + 2), u, y + 2)

    lax.fori_loop(1, ya - 1, lambda y, c: (first_step(y), c)[1], 0)

    lanes_o[...] = jnp.zeros_like(lanes_o)
    lanes_o[:, 0:xo] = sea2
    kap_rows[:, 0:xo] = kap_o[...]

    def sea_step(y):
        c = o[y + 1]
        kap = kap_rows[pl.ds(y, 1), :]
        wet = lanes_o[pl.ds(y, 1), :]
        beside = o[y] + o[y + 2] + pltpu.roll(c, 1, 1) + pltpu.roll(c, xop - 1, 1)
        o2[y] = c + wet * (kap * (beside - 4.0 * c) + split_product(mat_o[...], c))

    lax.fori_loop(1, yo - 1, lambda y, c: (sea_step(y), c)[1], 0)

    @pl.when(has_prev)
    def _():
        air_up.wait_recv()

    @pl.when(jnp.logical_not(has_prev))
    def _():
        u[0:2] = jnp.zeros((2, lap, xa), jnp.float32)

    @pl.when(has_next)
    def _():
        air_down.wait_recv()

    @pl.when(jnp.logical_not(has_next))
    def _():
        u[ya + 2 : ya + 4] = jnp.zeros((2, lap, xa), jnp.float32)

    for y in (-1, 0, ya - 1, ya):
        first_step(y)

    u2_copies = []
    for i in range(groups):
        lax.fori_loop(
            8 * i,
            8 * i + 8,
            lambda y, c: (air_step(u2, (y, y + 2), u1, y + 1), c)[1],
            0,
        )
        copy = pltpu.make_async_copy(
            u2.at[pl.ds(8 * i, 8)], u2_out.at[pl.ds(8 * i, 8)], dma.at[1 + i]
        )
        copy.start()
        u2_copies.append(copy)

    @pl.when(has_prev)
    def _():
        sea_up.wait_recv()

    @pl.when(jnp.logical_not(has_prev))
    def _():
        o[0] = jnp.zeros((lop, xop), jnp.float32)

    @pl.when(has_next)
    def _():
        sea_down.wait_recv()

    @pl.when(jnp.logical_not(has_next))
    def _():
        o[yo + 1] = jnp.zeros((lop, xop), jnp.float32)

    sea_step(0)
    sea_step(yo - 1)
    o2_copy = pltpu.make_async_copy(o2, o2_out, dma.at[0])
    o2_copy.start()

    for c in wgt_copies:
        c.wait()
    for q in range(1, nw):
        w_copies[q].wait_recv()
    for q in range(1, nf):
        f_copies[q].wait_recv()

    def combine(count, recv, wbuf, terms, tgt, cnt, row, rows):
        for q in range(count):
            s = source_of(q)
            live = lane_iota((1, cap)) < cnt[0, s]
            eff[row : row + 1, cap * q : cap * (q + 1)] = jnp.where(live, tgt[0, pl.ds(s, 1), :], -1)
            value = wbuf[q] * recv[q]
            high = value.astype(jnp.bfloat16)
            terms[cap * q : cap * (q + 1), 0:LANES] = high
            terms[cap * q : cap * (q + 1), LANES:] = (value - high.astype(jnp.float32)).astype(jnp.bfloat16)
        slots = cap * count
        chosen = eff[row : row + 1, 0:slots] == lax.broadcasted_iota(jnp.int32, (rows, slots), 0)
        onehot = jnp.where(chosen, 1.0, 0.0).astype(jnp.bfloat16)
        both = jnp.dot(onehot, terms[...], preferred_element_type=jnp.float32)
        return both[:, :LANES] + both[:, LANES:]

    r_a[...] = combine(nw, w_recv, w_wbuf, w_terms, w_tgt, w_cnt, 0, r_a.shape[0]) * AIR_EXCHANGER

    @pl.when(has_next)
    def _():
        blk_up.start()

    @pl.when(has_prev)
    def _():
        blk_down.start()

    r_o[...] = combine(nf, f_recv, f_wbuf, f_terms, f_tgt, f_cnt, 1, r_o.shape[0]) * COUPLE_OCEAN
    for y in range(yo):
        first, shift = (y * xo) // LANES, (y * xo) % LANES
        here = r_o[first : first + jo, :]
        if shift:
            after = r_o[first + 1 : first + jo + 1, :]
            here = jnp.where(
                lane_iota((jo, LANES)) < LANES - shift,
                pltpu.roll(here, LANES - shift, 1),
                pltpu.roll(after, LANES - shift, 1),
            )
        t_o[y * jo : (y + 1) * jo, :] = here
    for j in range(jo):
        cut = slice(j * LANES, (j + 1) * LANES)
        fl_out[:, cut] = t_o[pl.ds(j, yo, stride=jo), :] * lanes_o[:, cut]

    for j in range(ja):
        g_rows[8 : 8 + ya, j * LANES : (j + 1) * LANES] = r_a[pl.ds(j, ya, stride=ja), :]
    g_rows[0:8, :] = jnp.zeros((8, xa), jnp.float32)
    g_rows[8 + ya : 16 + ya, :] = jnp.zeros((8, xa), jnp.float32)

    @pl.when(has_prev)
    def _():
        blk_up.wait_recv()
        for j in range(ja):
            g_rows[7:8, j * LANES : (j + 1) * LANES] = r_halo[0, 16 - ja + j : 17 - ja + j, :]

    @pl.when(has_next)
    def _():
        blk_down.wait_recv()
        for j in range(ja):
            g_rows[8 + ya : 9 + ya, j * LANES : (j + 1) * LANES] = r_halo[1, j : j + 1, :]

    g = g_rows[8 : 8 + ya, :]
    g_out[...] = g
    beside = (
        g_rows[7 : 7 + ya, :]
        + g_rows[9 : 9 + ya, :]
        + pltpu.roll(g, 1, 1)
        + pltpu.roll(g, xa - 1, 1)
    )
    d_out[...] = kap_a[...] * (beside - 4.0 * g) + g

    for c in u2_copies:
        c.wait()
    o2_copy.wait()
    for q in range(1, nw):
        w_copies[q].wait_send()
    for q in range(1, nf):
        f_copies[q].wait_send()

    @pl.when(has_next)
    def _():
        air_up.wait_send()
        sea_up.wait_send()
        blk_up.wait_send()

    @pl.when(has_prev)
    def _():
        air_down.wait_send()
        sea_down.wait_send()
        blk_down.wait_send()


def finish_kernel(la, lo, u2, g, d, column, o2, fl, air, sea, energy):
    turned = jnp.swapaxes(u2[...], 0, 1)
    warm = g[...]
    for k in range(la):
        level = turned[k] + column[k] * warm
        if k == la - 1:
            level = level + d[...]
            energy[...] = warm - AIR_EXCHANGER * level
        air[k] = level
    turned = jnp.swapaxes(o2[...], 0, 1)
    sea[0] = turned[0] + fl[...]
    for k in range(1, lo):
        sea[k] = turned[k]


def parts_of(matrix, rows):
    padded = jnp.pad(matrix, ((0, rows - matrix.shape[0]), (0, rows - matrix.shape[1])))
    high = lax.reduce_precision(padded, 8, 7)
    low = padded - high
    return jnp.concatenate([high, high, low], axis=1).astype(jnp.bfloat16)


def shards(
    tiles,
    atmos,
    water_anomaly,
    atm_flux,
    ocean_mask,
    air_mixing_numbers,
    ocean_kappa,
    air_vertical_operator,
    ocean_column,
    a2o_source,
    a2o_target,
    a2o_count,
    a2o_weight,
    water_air_provider,
    water_air_receiver,
    water_air_live_tally,
    water_air_overlay_share,
):
    la, ya, xa = atmos.shape
    lo, yo, xo = water_anomaly.shape
    cap = a2o_source.shape[2]
    air_blocks, sea_blocks = ya * xa // LANES, yo * xo // LANES
    nw = min(tiles, -(-ENTRIES * air_blocks // cap) + 1)
    nf = min(tiles, -(-ENTRIES * sea_blocks // cap) + 1)
    dims = (tiles, la, ya, xa, lo, yo, xo, cap, nf, nw)
    lap, lop = round_up(la + 1, 8), round_up(lo, 8)
    xop = round_up(xo, LANES)
    jo = xop // LANES

    level = jnp.arange(la)
    diagonal = jnp.where(level == la - 1, 1.0 - AIR_EXCHANGER, 1.0).astype(jnp.float32)
    step_matrix = air_vertical_operator + jnp.diag(diagonal)
    mat_a = parts_of(step_matrix, lap)
    mat_o = parts_of(ocean_column, lop)

    f32 = jnp.float32
    vm = pl.BlockSpec(memory_space=pltpu.VMEM)
    sm = pl.BlockSpec(memory_space=pltpu.SMEM)
    hb = pl.BlockSpec(memory_space=pl.ANY)
    S = jax.ShapeDtypeStruct
    u2, o2, g, d, fl = pl.pallas_call(
        functools.partial(exchange_kernel, dims),
        out_shape=(
            S((ya, lap, xa), f32),
            S((yo, lop, xop), f32),
            S((ya, xa), f32),
            S((ya, xa), f32),
            S((yo, xop), f32),
        ),
        in_specs=[hb, hb, vm, vm, vm, vm, vm, vm, sm, vm, sm, hb, sm, vm, sm, hb],
        out_specs=(hb, hb, vm, vm, vm),
        scratch_shapes=[
            pltpu.VMEM((ya // 8, la, 8, xa), f32),
            pltpu.VMEM((ya + 4, lap, xa), f32),
            pltpu.VMEM((ya + 2, lap, xa), f32),
            pltpu.VMEM((ya, lap, xa), f32),
            pltpu.VMEM((lo, yo, xo), f32),
            pltpu.VMEM((yo + 2, lop, xop), f32),
            pltpu.VMEM((yo, lop, xop), f32),
            pltpu.VMEM((yo, xo), f32),
            pltpu.VMEM((air_blocks, LANES), f32),
            pltpu.VMEM((round_up(sea_blocks + jo, 8), LANES), f32),
            pltpu.VMEM((nf - 1, cap, LANES), f32),
            pltpu.VMEM((nw - 1, cap, LANES), f32),
            pltpu.VMEM((nf, cap, LANES), f32),
            pltpu.VMEM((nw, cap, LANES), f32),
            pltpu.VMEM((nf, cap, LANES), f32),
            pltpu.VMEM((nw, cap, LANES), f32),
            pltpu.VMEM((8, round_up(cap * nw, LANES)), jnp.int32),
            pltpu.VMEM((nf * cap, 2 * LANES), jnp.bfloat16),
            pltpu.VMEM((nw * cap, 2 * LANES), jnp.bfloat16),
            pltpu.VMEM((air_blocks, LANES), f32),
            pltpu.VMEM((round_up(sea_blocks + 2, 8), LANES), f32),
            pltpu.VMEM((yo * jo, LANES), f32),
            pltpu.VMEM((2, 16, LANES), f32),
            pltpu.VMEM((ya + 16, xa), f32),
            pltpu.VMEM((yo, xop), f32),
            pltpu.VMEM((yo, xop), f32),
            pltpu.SemaphoreType.DMA((2 + ya // 8 + nw + nf,)),
            pltpu.SemaphoreType.DMA((nf - 1,)),
            pltpu.SemaphoreType.DMA((nf - 1,)),
            pltpu.SemaphoreType.DMA((nw - 1,)),
            pltpu.SemaphoreType.DMA((nw - 1,)),
            pltpu.SemaphoreType.DMA((6,)),
            pltpu.SemaphoreType.DMA((6,)),
        ],
        compiler_params=pltpu.CompilerParams(
            collective_id=0, has_side_effects=True, vmem_limit_bytes=VMEM_BYTES
        ),
    )(
        atmos, water_anomaly, atm_flux, ocean_mask, air_mixing_numbers, ocean_kappa, mat_a, mat_o,
        a2o_source, a2o_target, a2o_count, a2o_weight,
        water_air_provider, water_air_receiver, water_air_live_tally, water_air_overlay_share,
    )

    steps = ya // 8
    cut = round_up(-(-xop // steps), LANES)
    return pl.pallas_call(
        functools.partial(finish_kernel, la, lo),
        grid=(steps,),
        out_shape=(S((la, ya, xa), f32), S((lo, yo, xo), f32), S((ya, xa), f32)),
        in_specs=[
            pl.BlockSpec((8, lap, xa), lambda i: (i, 0, 0)),
            pl.BlockSpec((8, xa), lambda i: (i, 0)),
            pl.BlockSpec((8, xa), lambda i: (i, 0)),
            pl.BlockSpec(memory_space=pltpu.SMEM),
            pl.BlockSpec((yo, lop, cut), lambda i: (0, 0, i)),
            pl.BlockSpec((yo, cut), lambda i: (0, i)),
        ],
        out_specs=(
            pl.BlockSpec((la, 8, xa), lambda i: (0, i, 0)),
            pl.BlockSpec((lo, yo, cut), lambda i: (0, 0, i)),
            pl.BlockSpec((8, xa), lambda i: (i, 0)),
        ),
        compiler_params=pltpu.CompilerParams(vmem_limit_bytes=VMEM_BYTES),
    )(u2, g, d, step_matrix[:, la - 1], o2, fl)


def solution(mesh):
    placed = (
        P("members", "tiles", None),
        P("members", "tiles", None),
        P("tiles", "members"),
        P("tiles", None),
        P("tiles", None),
        P("tiles", None),
        P(),
        P(),
        P("tiles", None, None),
        P("tiles", None, None),
        P("tiles", None),
        P("tiles", None, None, None),
        P("tiles", None, None),
        P("tiles", None, None),
        P("tiles", None),
        P("tiles", None, None, None),
    )
    return jax.shard_map(
        functools.partial(shards, mesh.shape["tiles"]),
        mesh=mesh,
        in_specs=placed,
        out_specs=(P("members", "tiles", None), P("members", "tiles", None), P("tiles", "members")),
        check_vma=False,
    )
```

```python
import functools

import jax
import jax.numpy as jnp
from jax import lax
from jax.experimental import pallas as pl
from jax.experimental.pallas import tpu as pltpu
from jax.sharding import PartitionSpec as P

LANES = 128
ENTRIES = 2
AIR_EXCHANGER = 0.3
COUPLE_OCEAN = 0.5
VMEM_BYTES = 60 * 1024 * 1024


def round_up(value, unit):
    return -(-value // unit) * unit


def offsets_of(tiles, count):
    leading = [0, tiles - 1, tiles // 2]
    return (leading + [v for v in range(tiles) if v not in leading])[:count]


def split_product(matrix, cells):
    high = cells.astype(jnp.bfloat16).astype(jnp.float32)
    low = cells - high
    stacked = jnp.concatenate([high, low, high], axis=0).astype(jnp.bfloat16)
    return jnp.dot(matrix, stacked, preferred_element_type=jnp.float32)


def lane_iota(shape):
    return lax.broadcasted_iota(jnp.int32, shape, len(shape) - 1)


def exchange_kernel(
    dims,
    atmos, water, flux_in, mask_in, kap_a_in, kap_o_in, op_a_in, op_o_in,
    f_src_in, f_tgt_in, f_cnt_in, f_wgt, w_src_in, w_tgt_in, w_cnt_in, w_wgt,
    u2_out, o2_out, g_out, d_out, fl_out,
    flux, mask, kap_a, kap_o, op_a, op_o, f_src, f_tgt, f_cnt, w_src, w_tgt, w_cnt,
    wide_a, wide_o, mat_a, mat_o,
    in_a, u, u1, u2, in_o, o, o2, surf,
    f_blocks, w_blocks, f_send, w_send, f_recv, w_recv, f_wbuf, w_wbuf,
    eff, f_terms, w_terms, r_a, r_o, t_o, r_halo, g_rows, lanes_o, kap_rows,
    dma, small, f_ss, f_rs, w_ss, w_rs, h_ss, h_rs,
):
    n, la, ya, xa, lo, yo, xo, cap, nf, nw = dims
    lap, lop = round_up(la + 1, 8), round_up(lo, 8)
    xop = round_up(xo, LANES)
    tail = xo % LANES
    ja, jo = xa // LANES, xop // LANES
    me = lax.axis_index("tiles")
    offs = offsets_of(n, nw)

    def source_of(q):
        return lax.rem(me + offs[q], n)

    def dest_of(q):
        return lax.rem(me + (n - offs[q]), n)

    barrier = pltpu.get_barrier_semaphore()
    for q in range(1, nw):
        pl.semaphore_signal(barrier, inc=1, device_id={"tiles": source_of(q)})

    small_copies = [
        pltpu.make_async_copy(src, dst, small.at[k])
        for k, (src, dst) in enumerate(
            (
                (mask_in, mask), (w_src_in, w_src), (flux_in, flux), (f_src_in, f_src),
                (kap_a_in, kap_a), (kap_o_in, kap_o), (op_a_in, op_a), (op_o_in, op_o),
                (f_tgt_in, f_tgt), (w_tgt_in, w_tgt), (f_cnt_in, f_cnt), (w_cnt_in, w_cnt),
            )
        )
    ]
    surf_copy = pltpu.make_async_copy(water.at[0], surf, dma.at[0])
    surf_copy.start()
    for c in small_copies:
        c.start()
    groups = ya // 8
    air_copies = [
        pltpu.make_async_copy(atmos.at[:, pl.ds(8 * i, 8), :], in_a.at[i], dma.at[1 + i])
        for i in range(groups)
    ]
    order = [0, groups - 1] + list(range(1, groups - 1))
    for i in order:
        air_copies[i].start()
    at = 1 + groups
    water_copy = pltpu.make_async_copy(water, in_o, dma.at[at])
    water_copy.start()
    at += 1
    wgt_copies = []
    for q in range(nw):
        wgt_copies.append(pltpu.make_async_copy(w_wgt.at[0, source_of(q)], w_wbuf.at[q], dma.at[at]))
        at += 1
    for q in range(nf):
        wgt_copies.append(pltpu.make_async_copy(f_wgt.at[0, source_of(q)], f_wbuf.at[q], dma.at[at]))
        at += 1
    for c in wgt_copies:
        c.start()

    surf_copy.wait()
    for c in small_copies[:4]:
        c.wait()
    for j in range(ja):
        f_blocks[pl.ds(j, ya, stride=ja), :] = flux[:, j * LANES : (j + 1) * LANES]
    sea2 = mask[...].astype(jnp.float32)
    lanes_o[...] = jnp.zeros_like(lanes_o)
    lanes_o[:, 0:xo] = surf[...] * sea2
    w_blocks[...] = jnp.zeros_like(w_blocks)
    for j in range(jo):
        t_o[pl.ds(j, yo, stride=jo), :] = lanes_o[:, j * LANES : (j + 1) * LANES]
    for y in range(yo):
        first, shift = (y * xo) // LANES, (y * xo) % LANES
        tiles = t_o[y * jo : (y + 1) * jo, :]
        if shift == 0:
            w_blocks[first : first + jo, :] = tiles
        else:
            rolled = pltpu.roll(tiles, shift, 1)
            before = jnp.concatenate([w_blocks[first : first + 1, :], rolled[: jo - 1]], axis=0)
            w_blocks[first : first + jo, :] = jnp.where(
                lane_iota((jo, LANES)) < shift, before, rolled
            )

    def gather(dst, blocks, source, d):
        def body(i, carry):
            for k in range(8):
                c = i * 8 + k
                dst[pl.ds(c, 1), :] = blocks[pl.ds(source[0, d, c], 1), :]
            return carry

        lax.fori_loop(0, cap // 8, body, 0)

    for q in range(nw):
        gather(w_recv.at[0] if q == 0 else w_send.at[q - 1], w_blocks, w_src, dest_of(q))
    for q in range(nf):
        gather(f_recv.at[0] if q == 0 else f_send.at[q - 1], f_blocks, f_src, dest_of(q))

    pl.semaphore_wait(barrier, nw - 1)
    w_copies, f_copies = {}, {}
    for q in range(1, nw):
        w_copies[q] = pltpu.make_async_remote_copy(
            src_ref=w_send.at[q - 1], dst_ref=w_recv.at[q],
            send_sem=w_ss.at[q - 1], recv_sem=w_rs.at[q - 1], device_id={"tiles": dest_of(q)},
        )
    for q in range(1, nf):
        f_copies[q] = pltpu.make_async_remote_copy(
            src_ref=f_send.at[q - 1], dst_ref=f_recv.at[q],
            send_sem=f_ss.at[q - 1], recv_sem=f_rs.at[q - 1], device_id={"tiles": dest_of(q)},
        )
    for q in [2] + list(range(nw - 1, 2, -1)) + [1]:
        w_copies[q].start()
        if q in f_copies:
            f_copies[q].start()

    for c in small_copies[4:]:
        c.wait()
    step = op_a[...]
    row = lax.broadcasted_iota(jnp.int32, (la, la), 0)
    keep = jnp.where(row == la - 1, 1.0 - AIR_EXCHANGER, 1.0)
    step = step + jnp.where(row == lane_iota((la, la)), keep, 0.0)
    for wide, out, matrix, size in ((wide_a, mat_a, step, lap), (wide_o, mat_o, op_o[...], lop)):
        side = matrix.shape[0]
        high = matrix.astype(jnp.bfloat16).astype(jnp.float32)
        wide[...] = jnp.zeros_like(wide)
        wide[0:side, 0:side] = high
        wide[0:side, size : size + side] = high
        wide[0:side, 2 * size : 2 * size + side] = matrix - high
        out[...] = wide[...].astype(jnp.bfloat16)

    kap_rows[...] = jnp.zeros_like(kap_rows)

    def turn_air(i):
        air_copies[i].wait()
        for j in range(ja):
            cut = pl.ds(j * LANES, LANES)
            u[pl.ds(2 + 8 * i, 8), 0:la, cut] = jnp.swapaxes(in_a[i, :, :, cut], 0, 1)
        for r in range(8):
            u[2 + 8 * i + r, la : la + 1, :] = kap_a[8 * i + r : 8 * i + r + 1, :]
            if lap > la + 1:
                u[2 + 8 * i + r, la + 1 : lap, :] = jnp.zeros((lap - la - 1, xa), jnp.float32)

    up, down = lax.rem(me + 1, n), lax.rem(me + n - 1, n)

    def to_next(k, src, dst):
        return pltpu.make_async_remote_copy(
            src_ref=src, dst_ref=dst, send_sem=h_ss.at[k], recv_sem=h_rs.at[k],
            device_id={"tiles": up},
        )

    def to_prev(k, src, dst):
        return pltpu.make_async_remote_copy(
            src_ref=src, dst_ref=dst, send_sem=h_ss.at[k], recv_sem=h_rs.at[k],
            device_id={"tiles": down},
        )

    has_next, has_prev = me < n - 1, me > 0
    air_up = to_next(0, u.at[pl.ds(ya, 2)], u.at[pl.ds(0, 2)])
    air_down = to_prev(1, u.at[pl.ds(2, 2)], u.at[pl.ds(ya + 2, 2)])
    sea_up = to_next(2, o.at[yo], o.at[0])
    sea_down = to_prev(3, o.at[1], o.at[yo + 1])
    blk_up = to_next(4, r_a.at[pl.ds(ya * ja - 16, 16)], r_halo.at[0])
    blk_down = to_prev(5, r_a.at[pl.ds(0, 16)], r_halo.at[1])

    turn_air(0)

    @pl.when(has_prev)
    def _():
        air_down.start()

    turn_air(groups - 1)

    @pl.when(has_next)
    def _():
        air_up.start()

    water_copy.wait()
    for j in range(jo):
        width = min(LANES, xo - j * LANES)
        cut = pl.ds(j * LANES, width)
        o[pl.ds(1, yo), 0:lo, cut] = jnp.swapaxes(in_o[:, :, cut], 0, 1)
    for y in range(yo):
        o[1 + y, lo:lop, :] = jnp.zeros((lop - lo, xop), jnp.float32)
        head = o[1 + y, :, 0:LANES]
        last = o[1 + y, :, xop - LANES : xop]
        lane = lane_iota((lop, LANES))
        wrapped = jnp.where(
            lane == tail,
            pltpu.roll(head, tail, 1),
            jnp.where(lane == LANES - 1, pltpu.roll(last, LANES - tail, 1), 0.0),
        )
        o[1 + y, :, xop - LANES : xop] = jnp.where(lane < tail, last, wrapped)

    @pl.when(has_prev)
    def _():
        sea_down.start()

    @pl.when(has_next)
    def _():
        sea_up.start()

    for i in range(1, groups - 1):
        turn_air(i)

    def air_step(dst, dst_row, src, row):
        c = src[row]
        kap = u[dst_row[1], la : la + 1, :]
        beside = src[row - 1] + src[row + 1] + pltpu.roll(c, 1, 1) + pltpu.roll(c, xa - 1, 1)
        dst[dst_row[0]] = split_product(mat_a[...], c) + kap * (beside - 4.0 * c)

    def first_step(y):
        air_step(u1, (y + 1, y + 2), u, y + 2)

    def rows_loop(start, stop, unroll, row_step):
        def body(k, carry):
            for r in range(unroll):
                row_step(start + k * unroll + r)
            return carry

        whole = (stop - start) // unroll
        lax.fori_loop(0, whole, body, 0)
        for y in range(start + whole * unroll, stop):
            row_step(y)

    rows_loop(1, ya - 1, 4, first_step)

    lanes_o[...] = jnp.zeros_like(lanes_o)
    lanes_o[:, 0:xo] = sea2
    kap_rows[:, 0:xo] = kap_o[...]

    def sea_step(y):
        c = o[y + 1]
        kap = kap_rows[pl.ds(y, 1), :]
        wet = lanes_o[pl.ds(y, 1), :]
        beside = o[y] + o[y + 2] + pltpu.roll(c, 1, 1) + pltpu.roll(c, xop - 1, 1)
        o2[y] = c + wet * (kap * (beside - 4.0 * c) + split_product(mat_o[...], c))

    rows_loop(1, yo - 1, 2, sea_step)

    @pl.when(has_prev)
    def _():
        air_up.wait_recv()

    @pl.when(jnp.logical_not(has_prev))
    def _():
        u[0:2] = jnp.zeros((2, lap, xa), jnp.float32)

    @pl.when(has_next)
    def _():
        air_down.wait_recv()

    @pl.when(jnp.logical_not(has_next))
    def _():
        u[ya + 2 : ya + 4] = jnp.zeros((2, lap, xa), jnp.float32)

    for y in (-1, 0, ya - 1, ya):
        first_step(y)

    out_copies = []
    for i in range(groups):
        rows_loop(8 * i, 8 * i + 8, 4, lambda y: air_step(u2, (y, y + 2), u1, y + 1))
        rows = pl.ds(8 * i, 8)
        out_copies.append(pltpu.make_async_copy(u2.at[rows], u2_out.at[rows], dma.at[1 + i]))
        out_copies[-1].start()

    @pl.when(has_prev)
    def _():
        sea_up.wait_recv()

    @pl.when(jnp.logical_not(has_prev))
    def _():
        o[0] = jnp.zeros((lop, xop), jnp.float32)

    @pl.when(has_next)
    def _():
        sea_down.wait_recv()

    @pl.when(jnp.logical_not(has_next))
    def _():
        o[yo + 1] = jnp.zeros((lop, xop), jnp.float32)

    sea_step(0)
    sea_step(yo - 1)
    out_copies.append(pltpu.make_async_copy(o2, o2_out, dma.at[0]))
    out_copies[-1].start()

    for c in wgt_copies:
        c.wait()
    for q in range(1, nw):
        w_copies[q].wait_recv()
    for q in range(1, nf):
        f_copies[q].wait_recv()

    def combine(count, recv, wbuf, terms, tgt, cnt, row, rows):
        for q in range(count):
            s = source_of(q)
            live = lane_iota((1, cap)) < cnt[0, s]
            eff[row : row + 1, cap * q : cap * (q + 1)] = jnp.where(live, tgt[0, pl.ds(s, 1), :], -1)
            value = wbuf[q] * recv[q]
            high = value.astype(jnp.bfloat16)
            terms[cap * q : cap * (q + 1), 0:LANES] = high
            terms[cap * q : cap * (q + 1), LANES:] = (value - high.astype(jnp.float32)).astype(jnp.bfloat16)
        slots = cap * count
        chosen = eff[row : row + 1, 0:slots] == lax.broadcasted_iota(jnp.int32, (rows, slots), 0)
        onehot = jnp.where(chosen, 1.0, 0.0).astype(jnp.bfloat16)
        both = jnp.dot(onehot, terms[...], preferred_element_type=jnp.float32)
        return both[:, :LANES] + both[:, LANES:]

    r_a[...] = combine(nw, w_recv, w_wbuf, w_terms, w_tgt, w_cnt, 0, r_a.shape[0]) * AIR_EXCHANGER

    @pl.when(has_next)
    def _():
        blk_up.start()

    @pl.when(has_prev)
    def _():
        blk_down.start()

    r_o[...] = combine(nf, f_recv, f_wbuf, f_terms, f_tgt, f_cnt, 1, r_o.shape[0]) * COUPLE_OCEAN
    for y in range(yo):
        first, shift = (y * xo) // LANES, (y * xo) % LANES
        here = r_o[first : first + jo, :]
        if shift:
            after = r_o[first + 1 : first + jo + 1, :]
            here = jnp.where(
                lane_iota((jo, LANES)) < LANES - shift,
                pltpu.roll(here, LANES - shift, 1),
                pltpu.roll(after, LANES - shift, 1),
            )
        t_o[y * jo : (y + 1) * jo, :] = here
    for j in range(jo):
        cut = slice(j * LANES, (j + 1) * LANES)
        fl_out[:, cut] = t_o[pl.ds(j, yo, stride=jo), :] * lanes_o[:, cut]

    for j in range(ja):
        g_rows[8 : 8 + ya, j * LANES : (j + 1) * LANES] = r_a[pl.ds(j, ya, stride=ja), :]
    g_rows[0:8, :] = jnp.zeros((8, xa), jnp.float32)
    g_rows[8 + ya : 16 + ya, :] = jnp.zeros((8, xa), jnp.float32)

    @pl.when(has_prev)
    def _():
        blk_up.wait_recv()
        for j in range(ja):
            g_rows[7:8, j * LANES : (j + 1) * LANES] = r_halo[0, 16 - ja + j : 17 - ja + j, :]

    @pl.when(has_next)
    def _():
        blk_down.wait_recv()
        for j in range(ja):
            g_rows[8 + ya : 9 + ya, j * LANES : (j + 1) * LANES] = r_halo[1, j : j + 1, :]

    g = g_rows[8 : 8 + ya, :]
    g_out[...] = g
    beside = (
        g_rows[7 : 7 + ya, :]
        + g_rows[9 : 9 + ya, :]
        + pltpu.roll(g, 1, 1)
        + pltpu.roll(g, xa - 1, 1)
    )
    d_out[...] = kap_a[...] * (beside - 4.0 * g) + g

    for c in out_copies:
        c.wait()
    for q in range(1, nw):
        w_copies[q].wait_send()
    for q in range(1, nf):
        f_copies[q].wait_send()

    @pl.when(has_next)
    def _():
        air_up.wait_send()
        sea_up.wait_send()
        blk_up.wait_send()

    @pl.when(has_prev)
    def _():
        air_down.wait_send()
        sea_down.wait_send()
        blk_down.wait_send()


def finish_kernel(
    dims,
    u2_in, g_in, d_in, op_a_in, o2_in, fl_in, air_out, sea_out, energy,
    u2, g, d, op_a, o2, fl, air, sea, in_sem, sem,
):
    n, la, ya, xa, lo, yo, xo, cap, nf, nw = dims
    groups = ya // 8
    arrivals = [
        pltpu.make_async_copy(src, dst, in_sem.at[groups + k])
        for k, (src, dst) in enumerate(
            ((g_in, g), (d_in, d), (op_a_in, op_a), (fl_in, fl), (o2_in, o2))
        )
    ]
    levels = [
        pltpu.make_async_copy(u2_in.at[pl.ds(8 * i, 8)], u2.at[pl.ds(8 * i, 8)], in_sem.at[i])
        for i in range(groups)
    ]
    for c in arrivals[:3] + levels + arrivals[3:]:
        c.start()
    for c in arrivals[:3]:
        c.wait()
    copies = []

    def send(src, dst):
        copies.append(pltpu.make_async_copy(src, dst, sem.at[len(copies)]))
        copies[-1].start()

    for i in range(groups):
        rows = pl.ds(8 * i, 8)
        levels[i].wait()
        for j in range(xa // LANES):
            cut = pl.ds(j * LANES, LANES)
            turned = jnp.swapaxes(u2[rows, :, cut], 0, 1)
            warm = g[rows, cut]
            for k in range(la):
                level = turned[k] + op_a[k : k + 1, la - 1 : la] * warm
                if k == la - 1:
                    level = level + (d[rows, cut] + (1.0 - AIR_EXCHANGER) * warm)
                    energy[rows, cut] = warm - AIR_EXCHANGER * level
                air[i, k, :, cut] = level
        send(air.at[i], air_out.at[:, rows, :])
    for c in arrivals[3:]:
        c.wait()
    for j in range(-(-xo // LANES)):
        width = min(LANES, xo - j * LANES)
        cut = pl.ds(j * LANES, width)
        turned = jnp.swapaxes(o2[:, :, cut], 0, 1)
        sea[0, :, cut] = turned[0] + fl[:, cut]
        sea[1:lo, :, cut] = turned[1:lo]
        edge = (j + 1) * LANES
        if edge % 512 == 0 and edge < xo:
            part = pl.ds(edge - 512, 512)
            send(sea.at[:, :, part], sea_out.at[:, :, part])
    rest = (xo // 512) * 512
    send(sea.at[:, :, pl.ds(rest, xo - rest)], sea_out.at[:, :, pl.ds(rest, xo - rest)])
    for c in copies:
        c.wait()


def shards(
    tiles,
    atmos,
    water_anomaly,
    atm_flux,
    ocean_mask,
    air_mixing_numbers,
    ocean_kappa,
    air_vertical_operator,
    ocean_column,
    a2o_source,
    a2o_target,
    a2o_count,
    a2o_weight,
    water_air_provider,
    water_air_receiver,
    water_air_live_tally,
    water_air_overlay_share,
):
    la, ya, xa = atmos.shape
    lo, yo, xo = water_anomaly.shape
    cap = a2o_source.shape[2]
    air_blocks, sea_blocks = ya * xa // LANES, yo * xo // LANES
    nw = min(tiles, -(-ENTRIES * air_blocks // cap) + 1)
    nf = min(tiles, -(-ENTRIES * sea_blocks // cap) + 1)
    dims = (tiles, la, ya, xa, lo, yo, xo, cap, nf, nw)
    lap, lop = round_up(la + 1, 8), round_up(lo, 8)
    xop = round_up(xo, LANES)
    jo = xop // LANES

    f32 = jnp.float32
    vm = pl.BlockSpec(memory_space=pltpu.VMEM)
    hb = pl.BlockSpec(memory_space=pltpu.HBM)
    S = jax.ShapeDtypeStruct
    u2, o2, g, d, fl = pl.pallas_call(
        functools.partial(exchange_kernel, dims),
        out_shape=(
            S((ya, lap, xa), f32),
            S((yo, lop, xop), f32),
            S((ya, xa), f32),
            S((ya, xa), f32),
            S((yo, xop), f32),
        ),
        in_specs=[hb] * 16,
        out_specs=(hb, hb, vm, vm, vm),
        scratch_shapes=[
            pltpu.VMEM((ya, xa), f32),
            pltpu.VMEM((yo, xo), jnp.int32),
            pltpu.VMEM((ya, xa), f32),
            pltpu.VMEM((yo, xo), f32),
            pltpu.VMEM((la, la), f32),
            pltpu.VMEM((lo, lo), f32),
            pltpu.SMEM((1, tiles, cap), jnp.int32),
            pltpu.VMEM((1, tiles, cap), jnp.int32),
            pltpu.SMEM((1, tiles), jnp.int32),
            pltpu.SMEM((1, tiles, cap), jnp.int32),
            pltpu.VMEM((1, tiles, cap), jnp.int32),
            pltpu.SMEM((1, tiles), jnp.int32),
            pltpu.VMEM((lap, 3 * lap), f32),
            pltpu.VMEM((lop, 3 * lop), f32),
            pltpu.VMEM((lap, 3 * lap), jnp.bfloat16),
            pltpu.VMEM((lop, 3 * lop), jnp.bfloat16),
            pltpu.VMEM((ya // 8, la, 8, xa), f32),
            pltpu.VMEM((ya + 4, lap, xa), f32),
            pltpu.VMEM((ya + 2, lap, xa), f32),
            pltpu.VMEM((ya, lap, xa), f32),
            pltpu.VMEM((lo, yo, xo), f32),
            pltpu.VMEM((yo + 2, lop, xop), f32),
            pltpu.VMEM((yo, lop, xop), f32),
            pltpu.VMEM((yo, xo), f32),
            pltpu.VMEM((air_blocks, LANES), f32),
            pltpu.VMEM((round_up(sea_blocks + jo, 8), LANES), f32),
            pltpu.VMEM((nf - 1, cap, LANES), f32),
            pltpu.VMEM((nw - 1, cap, LANES), f32),
            pltpu.VMEM((nf, cap, LANES), f32),
            pltpu.VMEM((nw, cap, LANES), f32),
            pltpu.VMEM((nf, cap, LANES), f32),
            pltpu.VMEM((nw, cap, LANES), f32),
            pltpu.VMEM((8, round_up(cap * nw, LANES)), jnp.int32),
            pltpu.VMEM((nf * cap, 2 * LANES), jnp.bfloat16),
            pltpu.VMEM((nw * cap, 2 * LANES), jnp.bfloat16),
            pltpu.VMEM((air_blocks, LANES), f32),
            pltpu.VMEM((round_up(sea_blocks + 2, 8), LANES), f32),
            pltpu.VMEM((yo * jo, LANES), f32),
            pltpu.VMEM((2, 16, LANES), f32),
            pltpu.VMEM((ya + 16, xa), f32),
            pltpu.VMEM((yo, xop), f32),
            pltpu.VMEM((yo, xop), f32),
            pltpu.SemaphoreType.DMA((2 + ya // 8 + nw + nf,)),
            pltpu.SemaphoreType.DMA((12,)),
            pltpu.SemaphoreType.DMA((nf - 1,)),
            pltpu.SemaphoreType.DMA((nf - 1,)),
            pltpu.SemaphoreType.DMA((nw - 1,)),
            pltpu.SemaphoreType.DMA((nw - 1,)),
            pltpu.SemaphoreType.DMA((6,)),
            pltpu.SemaphoreType.DMA((6,)),
        ],
        compiler_params=pltpu.CompilerParams(
            collective_id=0, has_side_effects=True, vmem_limit_bytes=VMEM_BYTES
        ),
    )(
        atmos, water_anomaly, atm_flux, ocean_mask, air_mixing_numbers, ocean_kappa, air_vertical_operator, ocean_column,
        a2o_source, a2o_target, a2o_count, a2o_weight,
        water_air_provider, water_air_receiver, water_air_live_tally, water_air_overlay_share,
    )

    return pl.pallas_call(
        functools.partial(finish_kernel, dims),
        out_shape=(S((la, ya, xa), f32), S((lo, yo, xo), f32), S((ya, xa), f32)),
        in_specs=[hb] * 6,
        out_specs=(hb, hb, vm),
        scratch_shapes=[
            pltpu.VMEM((ya, lap, xa), f32),
            pltpu.VMEM((ya, xa), f32),
            pltpu.VMEM((ya, xa), f32),
            pltpu.VMEM((la, la), f32),
            pltpu.VMEM((yo, lop, xop), f32),
            pltpu.VMEM((yo, xop), f32),
            pltpu.VMEM((ya // 8, la, 8, xa), f32),
            pltpu.VMEM((lo, yo, xo), f32),
            pltpu.SemaphoreType.DMA((ya // 8 + 5,)),
            pltpu.SemaphoreType.DMA((ya // 8 + xo // 512 + 1,)),
        ],
        compiler_params=pltpu.CompilerParams(vmem_limit_bytes=VMEM_BYTES),
    )(u2, g, d, air_vertical_operator, o2, fl)


def solution(mesh):
    placed = (
        P("members", "tiles", None),
        P("members", "tiles", None),
        P("tiles", "members"),
        P("tiles", None),
        P("tiles", None),
        P("tiles", None),
        P(),
        P(),
        P("tiles", None, None),
        P("tiles", None, None),
        P("tiles", None),
        P("tiles", None, None, None),
        P("tiles", None, None),
        P("tiles", None, None),
        P("tiles", None),
        P("tiles", None, None, None),
    )
    return jax.shard_map(
        functools.partial(shards, mesh.shape["tiles"]),
        mesh=mesh,
        in_specs=placed,
        out_specs=(P("members", "tiles", None), P("members", "tiles", None), P("tiles", "members")),
        check_vma=False,
    )
```

```python
import functools

import jax
import jax.numpy as jnp
from jax import lax
from jax.experimental import pallas as pl
from jax.experimental.pallas import tpu as pltpu
from jax.sharding import PartitionSpec as P

LANES = 128
ENTRIES = 2
AIR_EXCHANGER = 0.3
COUPLE_OCEAN = 0.5
VMEM_BYTES = 60 * 1024 * 1024


def round_up(value, unit):
    return -(-value // unit) * unit


def offsets_of(tiles, count):
    leading = [0, tiles - 1, tiles // 2]
    return (leading + [v for v in range(tiles) if v not in leading])[:count]


def split_product(matrix, cells):
    high = cells.astype(jnp.bfloat16).astype(jnp.float32)
    low = cells - high
    stacked = jnp.concatenate([high, low, high], axis=0).astype(jnp.bfloat16)
    return jnp.dot(matrix, stacked, preferred_element_type=jnp.float32)


def lane_iota(shape):
    return lax.broadcasted_iota(jnp.int32, shape, len(shape) - 1)


def exchange_kernel(
    dims,
    atmos, water, flux_in, mask_in, kap_a_in, kap_o_in, op_a_in, op_o_in,
    f_src_in, f_tgt_in, f_cnt_in, f_wgt, w_src_in, w_tgt_in, w_cnt_in, w_wgt,
    u2_out, o2_out, g_out, d_out, fl_out,
    flux, mask, kap_a, kap_o, op_a, op_o, f_src, f_tgt, f_cnt, w_src, w_tgt, w_cnt,
    wide_a, wide_o, mat_a, mat_o,
    in_a, u, u1, u2, in_o, o, o2, surf,
    f_blocks, w_blocks, f_send, w_send, f_recv, w_recv, f_wbuf, w_wbuf,
    eff, f_terms, w_terms, r_a, r_o, t_o, r_halo, g_rows, lanes_o, kap_rows,
    dma, small, f_ss, f_rs, w_ss, w_rs, h_ss, h_rs,
):
    n, la, ya, xa, lo, yo, xo, cap, nf, nw = dims
    lap, lop = round_up(la + 1, 8), round_up(lo, 8)
    xop = round_up(xo, LANES)
    tail = xo % LANES
    ja, jo = xa // LANES, xop // LANES
    me = lax.axis_index("tiles")
    offs = offsets_of(n, nw)

    def source_of(q):
        return lax.rem(me + offs[q], n)

    def dest_of(q):
        return lax.rem(me + (n - offs[q]), n)

    barrier = pltpu.get_barrier_semaphore()
    for q in range(1, nw):
        pl.semaphore_signal(barrier, inc=1, device_id={"tiles": source_of(q)})

    small_copies = [
        pltpu.make_async_copy(src, dst, small.at[k])
        for k, (src, dst) in enumerate(
            (
                (mask_in, mask), (w_src_in, w_src), (flux_in, flux), (f_src_in, f_src),
                (kap_a_in, kap_a), (kap_o_in, kap_o), (op_a_in, op_a), (op_o_in, op_o),
                (f_tgt_in, f_tgt), (w_tgt_in, w_tgt), (f_cnt_in, f_cnt), (w_cnt_in, w_cnt),
            )
        )
    ]
    surf_copy = pltpu.make_async_copy(water.at[0], surf, dma.at[0])
    surf_copy.start()
    for c in small_copies:
        c.start()
    groups = ya // 8
    air_copies = [
        pltpu.make_async_copy(atmos.at[:, pl.ds(8 * i, 8), :], in_a.at[i], dma.at[1 + i])
        for i in range(groups)
    ]
    order = [0, groups - 1] + list(range(1, groups - 1))
    for i in order:
        air_copies[i].start()
    at = 1 + groups
    water_copy = pltpu.make_async_copy(water, in_o, dma.at[at])
    water_copy.start()
    at += 1
    wgt_copies = []
    for q in range(nw):
        wgt_copies.append(pltpu.make_async_copy(w_wgt.at[0, source_of(q)], w_wbuf.at[q], dma.at[at]))
        at += 1
    for q in range(nf):
        wgt_copies.append(pltpu.make_async_copy(f_wgt.at[0, source_of(q)], f_wbuf.at[q], dma.at[at]))
        at += 1
    for c in wgt_copies:
        c.start()

    kap_rows[...] = jnp.zeros_like(kap_rows)

    def turn_air(i):
        air_copies[i].wait()
        for j in range(ja):
            cut = pl.ds(j * LANES, LANES)
            u[pl.ds(2 + 8 * i, 8), 0:la, cut] = jnp.swapaxes(in_a[i, :, :, cut], 0, 1)
        for r in range(8):
            u[2 + 8 * i + r, la : la + 1, :] = kap_a[8 * i + r : 8 * i + r + 1, :]
            if lap > la + 1:
                u[2 + 8 * i + r, la + 1 : lap, :] = jnp.zeros((lap - la - 1, xa), jnp.float32)

    up, down = lax.rem(me + 1, n), lax.rem(me + n - 1, n)

    def to_next(k, src, dst):
        return pltpu.make_async_remote_copy(
            src_ref=src, dst_ref=dst, send_sem=h_ss.at[k], recv_sem=h_rs.at[k],
            device_id={"tiles": up},
        )

    def to_prev(k, src, dst):
        return pltpu.make_async_remote_copy(
            src_ref=src, dst_ref=dst, send_sem=h_ss.at[k], recv_sem=h_rs.at[k],
            device_id={"tiles": down},
        )

    has_next, has_prev = me < n - 1, me > 0
    air_up = to_next(0, u.at[pl.ds(ya, 2)], u.at[pl.ds(0, 2)])
    air_down = to_prev(1, u.at[pl.ds(2, 2)], u.at[pl.ds(ya + 2, 2)])
    sea_up = to_next(2, o.at[yo], o.at[0])
    sea_down = to_prev(3, o.at[1], o.at[yo + 1])
    blk_up = to_next(4, r_a.at[pl.ds(ya * ja - 16, 16)], r_halo.at[0])
    blk_down = to_prev(5, r_a.at[pl.ds(0, 16)], r_halo.at[1])

    small_copies[4].wait()
    pl.semaphore_wait(barrier, nw - 1)
    turn_air(0)

    @pl.when(has_prev)
    def _():
        air_down.start()

    turn_air(groups - 1)

    @pl.when(has_next)
    def _():
        air_up.start()

    surf_copy.wait()
    for c in small_copies[:4]:
        c.wait()
    for j in range(ja):
        f_blocks[pl.ds(j, ya, stride=ja), :] = flux[:, j * LANES : (j + 1) * LANES]
    sea2 = mask[...].astype(jnp.float32)
    lanes_o[...] = jnp.zeros_like(lanes_o)
    lanes_o[:, 0:xo] = surf[...] * sea2
    w_blocks[...] = jnp.zeros_like(w_blocks)
    for j in range(jo):
        t_o[pl.ds(j, yo, stride=jo), :] = lanes_o[:, j * LANES : (j + 1) * LANES]
    for y in range(yo):
        first, shift = (y * xo) // LANES, (y * xo) % LANES
        tiles = t_o[y * jo : (y + 1) * jo, :]
        if shift == 0:
            w_blocks[first : first + jo, :] = tiles
        else:
            rolled = pltpu.roll(tiles, shift, 1)
            before = jnp.concatenate([w_blocks[first : first + 1, :], rolled[: jo - 1]], axis=0)
            w_blocks[first : first + jo, :] = jnp.where(
                lane_iota((jo, LANES)) < shift, before, rolled
            )

    def gather(dst, blocks, source, d):
        def body(i, carry):
            for k in range(8):
                c = i * 8 + k
                dst[pl.ds(c, 1), :] = blocks[pl.ds(source[0, d, c], 1), :]
            return carry

        lax.fori_loop(0, cap // 8, body, 0)

    for q in range(nw):
        gather(w_recv.at[0] if q == 0 else w_send.at[q - 1], w_blocks, w_src, dest_of(q))
    for q in range(nf):
        gather(f_recv.at[0] if q == 0 else f_send.at[q - 1], f_blocks, f_src, dest_of(q))

    w_copies, f_copies = {}, {}
    for q in range(1, nw):
        w_copies[q] = pltpu.make_async_remote_copy(
            src_ref=w_send.at[q - 1], dst_ref=w_recv.at[q],
            send_sem=w_ss.at[q - 1], recv_sem=w_rs.at[q - 1], device_id={"tiles": dest_of(q)},
        )
    for q in range(1, nf):
        f_copies[q] = pltpu.make_async_remote_copy(
            src_ref=f_send.at[q - 1], dst_ref=f_recv.at[q],
            send_sem=f_ss.at[q - 1], recv_sem=f_rs.at[q - 1], device_id={"tiles": dest_of(q)},
        )
    for q in [2] + list(range(nw - 1, 2, -1)) + [1]:
        w_copies[q].start()
        if q in f_copies:
            f_copies[q].start()

    water_copy.wait()
    for j in range(jo):
        width = min(LANES, xo - j * LANES)
        cut = pl.ds(j * LANES, width)
        o[pl.ds(1, yo), 0:lo, cut] = jnp.swapaxes(in_o[:, :, cut], 0, 1)
    for y in range(yo):
        o[1 + y, lo:lop, :] = jnp.zeros((lop - lo, xop), jnp.float32)
        head = o[1 + y, :, 0:LANES]
        last = o[1 + y, :, xop - LANES : xop]
        lane = lane_iota((lop, LANES))
        wrapped = jnp.where(
            lane == tail,
            pltpu.roll(head, tail, 1),
            jnp.where(lane == LANES - 1, pltpu.roll(last, LANES - tail, 1), 0.0),
        )
        o[1 + y, :, xop - LANES : xop] = jnp.where(lane < tail, last, wrapped)

    @pl.when(has_prev)
    def _():
        sea_down.start()

    @pl.when(has_next)
    def _():
        sea_up.start()

    for c in small_copies[5:]:
        c.wait()
    step = op_a[...]
    row = lax.broadcasted_iota(jnp.int32, (la, la), 0)
    keep = jnp.where(row == la - 1, 1.0 - AIR_EXCHANGER, 1.0)
    step = step + jnp.where(row == lane_iota((la, la)), keep, 0.0)
    for wide, out, matrix, size in ((wide_a, mat_a, step, lap), (wide_o, mat_o, op_o[...], lop)):
        side = matrix.shape[0]
        high = matrix.astype(jnp.bfloat16).astype(jnp.float32)
        wide[...] = jnp.zeros_like(wide)
        wide[0:side, 0:side] = high
        wide[0:side, size : size + side] = high
        wide[0:side, 2 * size : 2 * size + side] = matrix - high
        out[...] = wide[...].astype(jnp.bfloat16)

    for i in range(1, groups - 1):
        turn_air(i)

    def air_step(dst, dst_row, src, row):
        c = src[row]
        kap = u[dst_row[1], la : la + 1, :]
        beside = src[row - 1] + src[row + 1] + pltpu.roll(c, 1, 1) + pltpu.roll(c, xa - 1, 1)
        dst[dst_row[0]] = split_product(mat_a[...], c) + kap * (beside - 4.0 * c)

    def first_step(y):
        air_step(u1, (y + 1, y + 2), u, y + 2)

    def rows_loop(start, stop, unroll, row_step):
        def body(k, carry):
            for r in range(unroll):
                row_step(start + k * unroll + r)
            return carry

        whole = (stop - start) // unroll
        lax.fori_loop(0, whole, body, 0)
        for y in range(start + whole * unroll, stop):
            row_step(y)

    def second_step(y):
        air_step(u2, (y, y + 2), u1, y + 1)

    out_copies = []

    def hand_out(i):
        rows = pl.ds(8 * i, 8)
        out_copies.append(pltpu.make_async_copy(u2.at[rows], u2_out.at[rows], dma.at[1 + i]))
        out_copies[-1].start()

    rows_loop(1, ya - 1, 4, first_step)
    rows_loop(2, ya - 2, 4, second_step)
    for i in range(1, groups - 1):
        hand_out(i)

    lanes_o[...] = jnp.zeros_like(lanes_o)
    lanes_o[:, 0:xo] = sea2
    kap_rows[:, 0:xo] = kap_o[...]

    def sea_step(y):
        c = o[y + 1]
        kap = kap_rows[pl.ds(y, 1), :]
        wet = lanes_o[pl.ds(y, 1), :]
        beside = o[y] + o[y + 2] + pltpu.roll(c, 1, 1) + pltpu.roll(c, xop - 1, 1)
        o2[y] = c + wet * (kap * (beside - 4.0 * c) + split_product(mat_o[...], c))

    rows_loop(1, yo - 1, 2, sea_step)

    @pl.when(has_prev)
    def _():
        air_up.wait_recv()

    @pl.when(jnp.logical_not(has_prev))
    def _():
        u[0:2] = jnp.zeros((2, lap, xa), jnp.float32)

    @pl.when(has_next)
    def _():
        air_down.wait_recv()

    @pl.when(jnp.logical_not(has_next))
    def _():
        u[ya + 2 : ya + 4] = jnp.zeros((2, lap, xa), jnp.float32)

    for y in (-1, 0, ya - 1, ya):
        first_step(y)

    for y in (0, 1, ya - 2, ya - 1):
        second_step(y)
    hand_out(0)
    hand_out(groups - 1)

    for c in wgt_copies:
        c.wait()
    for q in range(1, nw):
        w_copies[q].wait_recv()
    for q in range(1, nf):
        f_copies[q].wait_recv()

    def combine(count, recv, wbuf, terms, tgt, cnt, row, rows):
        for q in range(count):
            s = source_of(q)
            live = lane_iota((1, cap)) < cnt[0, s]
            eff[row : row + 1, cap * q : cap * (q + 1)] = jnp.where(live, tgt[0, pl.ds(s, 1), :], -1)
            value = wbuf[q] * recv[q]
            high = value.astype(jnp.bfloat16)
            terms[cap * q : cap * (q + 1), 0:LANES] = high
            terms[cap * q : cap * (q + 1), LANES:] = (value - high.astype(jnp.float32)).astype(jnp.bfloat16)
        slots = cap * count
        chosen = eff[row : row + 1, 0:slots] == lax.broadcasted_iota(jnp.int32, (rows, slots), 0)
        onehot = jnp.where(chosen, 1.0, 0.0).astype(jnp.bfloat16)
        both = jnp.dot(onehot, terms[...], preferred_element_type=jnp.float32)
        return both[:, :LANES] + both[:, LANES:]

    r_a[...] = combine(nw, w_recv, w_wbuf, w_terms, w_tgt, w_cnt, 0, r_a.shape[0]) * AIR_EXCHANGER

    @pl.when(has_next)
    def _():
        blk_up.start()

    @pl.when(has_prev)
    def _():
        blk_down.start()

    r_o[...] = combine(nf, f_recv, f_wbuf, f_terms, f_tgt, f_cnt, 1, r_o.shape[0]) * COUPLE_OCEAN
    for y in range(yo):
        first, shift = (y * xo) // LANES, (y * xo) % LANES
        here = r_o[first : first + jo, :]
        if shift:
            after = r_o[first + 1 : first + jo + 1, :]
            here = jnp.where(
                lane_iota((jo, LANES)) < LANES - shift,
                pltpu.roll(here, LANES - shift, 1),
                pltpu.roll(after, LANES - shift, 1),
            )
        t_o[y * jo : (y + 1) * jo, :] = here
    for j in range(jo):
        cut = slice(j * LANES, (j + 1) * LANES)
        fl_out[:, cut] = t_o[pl.ds(j, yo, stride=jo), :] * lanes_o[:, cut]

    @pl.when(has_prev)
    def _():
        sea_up.wait_recv()

    @pl.when(jnp.logical_not(has_prev))
    def _():
        o[0] = jnp.zeros((lop, xop), jnp.float32)

    @pl.when(has_next)
    def _():
        sea_down.wait_recv()

    @pl.when(jnp.logical_not(has_next))
    def _():
        o[yo + 1] = jnp.zeros((lop, xop), jnp.float32)

    sea_step(0)
    sea_step(yo - 1)
    out_copies.append(pltpu.make_async_copy(o2, o2_out, dma.at[0]))
    out_copies[-1].start()

    for j in range(ja):
        g_rows[8 : 8 + ya, j * LANES : (j + 1) * LANES] = r_a[pl.ds(j, ya, stride=ja), :]
    g_rows[0:8, :] = jnp.zeros((8, xa), jnp.float32)
    g_rows[8 + ya : 16 + ya, :] = jnp.zeros((8, xa), jnp.float32)

    @pl.when(has_prev)
    def _():
        blk_up.wait_recv()
        for j in range(ja):
            g_rows[7:8, j * LANES : (j + 1) * LANES] = r_halo[0, 16 - ja + j : 17 - ja + j, :]

    @pl.when(has_next)
    def _():
        blk_down.wait_recv()
        for j in range(ja):
            g_rows[8 + ya : 9 + ya, j * LANES : (j + 1) * LANES] = r_halo[1, j : j + 1, :]

    g = g_rows[8 : 8 + ya, :]
    g_out[...] = g
    beside = (
        g_rows[7 : 7 + ya, :]
        + g_rows[9 : 9 + ya, :]
        + pltpu.roll(g, 1, 1)
        + pltpu.roll(g, xa - 1, 1)
    )
    d_out[...] = kap_a[...] * (beside - 4.0 * g) + g

    for c in out_copies:
        c.wait()
    for q in range(1, nw):
        w_copies[q].wait_send()
    for q in range(1, nf):
        f_copies[q].wait_send()

    @pl.when(has_next)
    def _():
        air_up.wait_send()
        sea_up.wait_send()
        blk_up.wait_send()

    @pl.when(has_prev)
    def _():
        air_down.wait_send()
        sea_down.wait_send()
        blk_down.wait_send()


def finish_kernel(
    dims,
    u2_in, g_in, d_in, op_a_in, o2_in, fl_in, air_out, sea_out, energy,
    u2, g, d, op_a, o2, fl, air, sea, in_sem, sem,
):
    n, la, ya, xa, lo, yo, xo, cap, nf, nw = dims
    groups = ya // 8
    arrivals = [
        pltpu.make_async_copy(src, dst, in_sem.at[groups + k])
        for k, (src, dst) in enumerate(
            ((g_in, g), (d_in, d), (op_a_in, op_a), (fl_in, fl), (o2_in, o2))
        )
    ]
    levels = [
        pltpu.make_async_copy(u2_in.at[pl.ds(8 * i, 8)], u2.at[pl.ds(8 * i, 8)], in_sem.at[i])
        for i in range(groups)
    ]
    for c in arrivals[:3] + levels + arrivals[3:]:
        c.start()
    for c in arrivals[:3]:
        c.wait()
    copies = []

    def send(src, dst):
        copies.append(pltpu.make_async_copy(src, dst, sem.at[len(copies)]))
        copies[-1].start()

    for i in range(groups):
        rows = pl.ds(8 * i, 8)
        levels[i].wait()
        for j in range(xa // LANES):
            cut = pl.ds(j * LANES, LANES)
            turned = jnp.swapaxes(u2[rows, :, cut], 0, 1)
            warm = g[rows, cut]
            for k in range(la):
                level = turned[k] + op_a[k : k + 1, la - 1 : la] * warm
                if k == la - 1:
                    level = level + (d[rows, cut] + (1.0 - AIR_EXCHANGER) * warm)
                    energy[rows, cut] = warm - AIR_EXCHANGER * level
                air[i, k, :, cut] = level
        send(air.at[i], air_out.at[:, rows, :])
    for c in arrivals[3:]:
        c.wait()
    for j in range(-(-xo // LANES)):
        width = min(LANES, xo - j * LANES)
        cut = pl.ds(j * LANES, width)
        turned = jnp.swapaxes(o2[:, :, cut], 0, 1)
        sea[0, :, cut] = turned[0] + fl[:, cut]
        sea[1:lo, :, cut] = turned[1:lo]
        edge = (j + 1) * LANES
        if edge % 512 == 0 and edge < xo:
            part = pl.ds(edge - 512, 512)
            send(sea.at[:, :, part], sea_out.at[:, :, part])
    rest = (xo // 512) * 512
    send(sea.at[:, :, pl.ds(rest, xo - rest)], sea_out.at[:, :, pl.ds(rest, xo - rest)])
    for c in copies:
        c.wait()


def shards(
    tiles,
    atmos,
    water_anomaly,
    atm_flux,
    ocean_mask,
    air_mixing_numbers,
    ocean_kappa,
    air_vertical_operator,
    ocean_column,
    a2o_source,
    a2o_target,
    a2o_count,
    a2o_weight,
    water_air_provider,
    water_air_receiver,
    water_air_live_tally,
    water_air_overlay_share,
):
    la, ya, xa = atmos.shape
    lo, yo, xo = water_anomaly.shape
    cap = a2o_source.shape[2]
    air_blocks, sea_blocks = ya * xa // LANES, yo * xo // LANES
    nw = min(tiles, -(-ENTRIES * air_blocks // cap) + 1)
    nf = min(tiles, -(-ENTRIES * sea_blocks // cap) + 1)
    dims = (tiles, la, ya, xa, lo, yo, xo, cap, nf, nw)
    lap, lop = round_up(la + 1, 8), round_up(lo, 8)
    xop = round_up(xo, LANES)
    jo = xop // LANES

    f32 = jnp.float32
    vm = pl.BlockSpec(memory_space=pltpu.VMEM)
    hb = pl.BlockSpec(memory_space=pltpu.HBM)
    S = jax.ShapeDtypeStruct
    u2, o2, g, d, fl = pl.pallas_call(
        functools.partial(exchange_kernel, dims),
        out_shape=(
            S((ya, lap, xa), f32),
            S((yo, lop, xop), f32),
            S((ya, xa), f32),
            S((ya, xa), f32),
            S((yo, xop), f32),
        ),
        in_specs=[hb] * 16,
        out_specs=(hb, hb, vm, vm, vm),
        scratch_shapes=[
            pltpu.VMEM((ya, xa), f32),
            pltpu.VMEM((yo, xo), jnp.int32),
            pltpu.VMEM((ya, xa), f32),
            pltpu.VMEM((yo, xo), f32),
            pltpu.VMEM((la, la), f32),
            pltpu.VMEM((lo, lo), f32),
            pltpu.SMEM((1, tiles, cap), jnp.int32),
            pltpu.VMEM((1, tiles, cap), jnp.int32),
            pltpu.SMEM((1, tiles), jnp.int32),
            pltpu.SMEM((1, tiles, cap), jnp.int32),
            pltpu.VMEM((1, tiles, cap), jnp.int32),
            pltpu.SMEM((1, tiles), jnp.int32),
            pltpu.VMEM((lap, 3 * lap), f32),
            pltpu.VMEM((lop, 3 * lop), f32),
            pltpu.VMEM((lap, 3 * lap), jnp.bfloat16),
            pltpu.VMEM((lop, 3 * lop), jnp.bfloat16),
            pltpu.VMEM((ya // 8, la, 8, xa), f32),
            pltpu.VMEM((ya + 4, lap, xa), f32),
            pltpu.VMEM((ya + 2, lap, xa), f32),
            pltpu.VMEM((ya, lap, xa), f32),
            pltpu.VMEM((lo, yo, xo), f32),
            pltpu.VMEM((yo + 2, lop, xop), f32),
            pltpu.VMEM((yo, lop, xop), f32),
            pltpu.VMEM((yo, xo), f32),
            pltpu.VMEM((air_blocks, LANES), f32),
            pltpu.VMEM((round_up(sea_blocks + jo, 8), LANES), f32),
            pltpu.VMEM((nf - 1, cap, LANES), f32),
            pltpu.VMEM((nw - 1, cap, LANES), f32),
            pltpu.VMEM((nf, cap, LANES), f32),
            pltpu.VMEM((nw, cap, LANES), f32),
            pltpu.VMEM((nf, cap, LANES), f32),
            pltpu.VMEM((nw, cap, LANES), f32),
            pltpu.VMEM((8, round_up(cap * nw, LANES)), jnp.int32),
            pltpu.VMEM((nf * cap, 2 * LANES), jnp.bfloat16),
            pltpu.VMEM((nw * cap, 2 * LANES), jnp.bfloat16),
            pltpu.VMEM((air_blocks, LANES), f32),
            pltpu.VMEM((round_up(sea_blocks + 2, 8), LANES), f32),
            pltpu.VMEM((yo * jo, LANES), f32),
            pltpu.VMEM((2, 16, LANES), f32),
            pltpu.VMEM((ya + 16, xa), f32),
            pltpu.VMEM((yo, xop), f32),
            pltpu.VMEM((yo, xop), f32),
            pltpu.SemaphoreType.DMA((2 + ya // 8 + nw + nf,)),
            pltpu.SemaphoreType.DMA((12,)),
            pltpu.SemaphoreType.DMA((nf - 1,)),
            pltpu.SemaphoreType.DMA((nf - 1,)),
            pltpu.SemaphoreType.DMA((nw - 1,)),
            pltpu.SemaphoreType.DMA((nw - 1,)),
            pltpu.SemaphoreType.DMA((6,)),
            pltpu.SemaphoreType.DMA((6,)),
        ],
        compiler_params=pltpu.CompilerParams(
            collective_id=0, has_side_effects=True, vmem_limit_bytes=VMEM_BYTES
        ),
    )(
        atmos, water_anomaly, atm_flux, ocean_mask, air_mixing_numbers, ocean_kappa, air_vertical_operator, ocean_column,
        a2o_source, a2o_target, a2o_count, a2o_weight,
        water_air_provider, water_air_receiver, water_air_live_tally, water_air_overlay_share,
    )

    return pl.pallas_call(
        functools.partial(finish_kernel, dims),
        out_shape=(S((la, ya, xa), f32), S((lo, yo, xo), f32), S((ya, xa), f32)),
        in_specs=[hb] * 6,
        out_specs=(hb, hb, vm),
        scratch_shapes=[
            pltpu.VMEM((ya, lap, xa), f32),
            pltpu.VMEM((ya, xa), f32),
            pltpu.VMEM((ya, xa), f32),
            pltpu.VMEM((la, la), f32),
            pltpu.VMEM((yo, lop, xop), f32),
            pltpu.VMEM((yo, xop), f32),
            pltpu.VMEM((ya // 8, la, 8, xa), f32),
            pltpu.VMEM((lo, yo, xo), f32),
            pltpu.SemaphoreType.DMA((ya // 8 + 5,)),
            pltpu.SemaphoreType.DMA((ya // 8 + xo // 512 + 1,)),
        ],
        compiler_params=pltpu.CompilerParams(vmem_limit_bytes=VMEM_BYTES),
    )(u2, g, d, air_vertical_operator, o2, fl)


def solution(mesh):
    placed = (
        P("members", "tiles", None),
        P("members", "tiles", None),
        P("tiles", "members"),
        P("tiles", None),
        P("tiles", None),
        P("tiles", None),
        P(),
        P(),
        P("tiles", None, None),
        P("tiles", None, None),
        P("tiles", None),
        P("tiles", None, None, None),
        P("tiles", None, None),
        P("tiles", None, None),
        P("tiles", None),
        P("tiles", None, None, None),
    )
    return jax.shard_map(
        functools.partial(shards, mesh.shape["tiles"]),
        mesh=mesh,
        in_specs=placed,
        out_specs=(P("members", "tiles", None), P("members", "tiles", None), P("tiles", "members")),
        check_vma=False,
    )
```
